512 devices in a mesh: phi: 128 (over x, y_hi, z, core), eta: 4 (over y_lo).
Axes of the slice: x: 4, y: 8 (y_hi: 2, y_lo: 4; y = y_hi * 4 + y_lo), z: 8, core: 2. Of those that a mesh axis runs over, the one named last changes fastest.
Arguments:
- noisy_field: bfloat16 [512, 256, 768], P('phi', 'eta'), may hold values from -6 to 6
- noise_draw: bfloat16 [512, 256, 768], P('phi', 'eta'), may hold values from -6 to 6
- coarse_latent: bfloat16 [2048, 512], P('phi'), may hold values from -6 to 6
- particle_type: int32 [2048], P('phi'), may hold values from 0 to 7
- type_table: bfloat16 [8, 512], replicated, may hold values from -6 to 6
- kv_weight: bfloat16 [512, 384], replicated, may hold values from -2.3864854 to 2.3864854
- norm_gain: float32 [2, 96], replicated, may hold values from 0.1 to 1.9
- conv_weight: bfloat16 [2, 9, 96, 96], replicated, may hold values from -0.21875 to 0.21875
- query_weight: bfloat16 [2, 96, 96], replicated, may hold values from -0.625 to 0.625
- mix_weight: bfloat16 [2, 96, 96], replicated, may hold values from -0.625 to 0.625
- out_weight: bfloat16 [2, 96, 96], replicated, may hold values from -0.15625 to 0.15625
Outputs:
- denoised: bfloat16 [512, 256, 768], P('phi', 'eta')
The draws below stay inside these ranges and needn't reach their ends.
All inputs are finite; a program needn't handle non-finite values.
Results may differ from the reference program's by a relative error of at most 0.0067.
Values may be sent and summed in bfloat16 or wider, within the bound.
No kernel may reach another device: no remote copies, remote signals or barrier semaphores. Data moves between devices by JAX's collectives and lax.ppermute only.
A program may use at most 64 MiB of HBM per device.

```python
import math
import jax
import jax.numpy as jnp
from jax import lax

C = 96
LATENT = 512
TYPES = 8
HEADS = 2
BLOCKS = 2
LAYERS = 8
HDIM = 48
NPHI = 512
NETA = 256
CTOK = 2048


def draw_kv_weight(key, part):
    key = jax.random.fold_in(key, 11)
    columns = jnp.arange(BLOCKS * 2 * C, dtype=jnp.int32)
    is_key = columns // C % 2 == 0
    column_scale = jnp.where(is_key, 2.2, 9.0).astype(jnp.float32) * LATENT ** (-0.5)
    base = jnp.clip(jax.random.normal(key, (LATENT, BLOCKS * 2 * C), jnp.float32), -6.0, 6.0)
    return (base * column_scale[None, :]).astype(jnp.bfloat16)


def plant(drawn, key, least, high):
    longest = drawn.shape.index(max(drawn.shape))
    spots = []
    for shift in (0, 1):
        where = [jax.random.randint(jax.random.fold_in(key, axis), (), 0, length) for axis, length in enumerate(drawn.shape)]
        where[longest] = (where[longest] + shift) % drawn.shape[longest]
        spots.append(tuple(where))
    return drawn.at[spots[0]].set(least).at[spots[1]].set(high)


def block_levels(own_key, extent, split, low, largest):
    factor_of = 1.0
    for position, blocks in split:
        draws = jax.random.uniform(jax.random.fold_in(jax.random.fold_in(own_key, 6), position), (blocks,), jnp.float32, low / len(split), largest / len(split))
        factor_of = factor_of * jnp.repeat(jnp.exp(draws), extent[position] // blocks).reshape((-1,) + (1,) * (len(extent) - 1 - position))
    return factor_of


def normal_values(rng, shape, scale, most, shards=(), kind=jnp.bfloat16):
    result = jax.random.normal(rng, shape, jnp.float32) * scale
    if len(shards) > 0:
        result = block_levels(rng, shape, shards, -0.22, 0.18) * result
    return jnp.clip(result, min=-most, max=most).astype(kind)


def setup_inputs(seed: int = 0) -> dict:
    keys = jax.random.split(jax.random.key(seed), 12)
    return {
        "noisy_field": normal_values(keys[0], (NPHI, NETA, LAYERS * C), 1.0, 6.0, ((0, 128), (1, 4))),
        "noise_draw": normal_values(keys[1], (NPHI, NETA, LAYERS * C), 1.0, 6.0, ((0, 128), (1, 4))),
        "coarse_latent": normal_values(keys[2], (CTOK, LATENT), 1.0, 6.0, ((0, 128),)),
        "particle_type": plant(jax.random.randint(keys[3], (CTOK,), 0, TYPES), jax.random.fold_in(keys[3], 1), 0, TYPES - 1).astype(jnp.int32),
        "type_table": normal_values(keys[4], (TYPES, LATENT), 1.0, 6.0),
        "kv_weight": draw_kv_weight(jax.random.fold_in(keys[11], 71), 0),
        "norm_gain": jnp.clip(1.0 + 0.18 * jax.random.normal(keys[6], (BLOCKS, C), jnp.float32), 0.1, 1.9),
        "conv_weight": normal_values(keys[7], (BLOCKS, 9, C, C), (9 * C) ** -0.5, 0.21875),
        "query_weight": normal_values(keys[8], (BLOCKS, C, C), C ** -0.5, 0.625),
        "mix_weight": normal_values(keys[9], (BLOCKS, C, C), C ** -0.5, 0.625),
        "out_weight": normal_values(keys[10], (BLOCKS, C, C), (16 * C) ** -0.5, 0.15625),
    }


eps = 1e-06

def coarse_keys(coarse_latent, particle_type, type_table, kv_weight):
    picked = (particle_type[:, None] == jnp.arange(TYPES, dtype=jnp.int32)[None, :]).astype(jnp.float32)
    embed = jnp.dot(picked, type_table.astype(jnp.float32))
    hidden = jax.nn.silu(coarse_latent.astype(jnp.float32) + embed).astype(jnp.bfloat16)
    return jnp.dot(hidden, kv_weight, preferred_element_type=jnp.float32).astype(jnp.bfloat16)

def convolve(padded, weight):
    span_p = padded.shape[0] - 2
    span_e = padded.shape[1] - 2
    summed = jnp.zeros((span_p, span_e) + padded.shape[2:], jnp.float32)
    for offset_row in range(3):
        for offset_col in range(3):
            shifted = padded[offset_row:offset_row + span_p, offset_col:offset_col + span_e].astype(jnp.float32)
            summed = summed + jnp.einsum('pelc,cd->peld', shifted, weight[3 * offset_row + offset_col].astype(jnp.float32))
    return summed

def attend(query, key_rows, value_rows):
    cell_count = query.shape[0]
    width = math.gcd(512, cell_count)
    grouped = query.reshape(cell_count // width, width, HEADS, HDIM)
    keyed = key_rows.reshape(-1, HEADS, HDIM).astype(jnp.float32)
    valued = value_rows.reshape(-1, HEADS, HDIM).astype(jnp.float32)
    score_scale = 1.0 / math.sqrt(HDIM)

    def one_group(rows):
        scores = jnp.einsum('bhd,thd->hbt', rows.astype(jnp.float32), keyed) * score_scale
        probs = jax.nn.softmax(scores, axis=-1).astype(jnp.bfloat16)
        return jnp.einsum('hbt,thd->bhd', probs.astype(jnp.float32), valued).astype(jnp.bfloat16)
    return lax.map(one_group, grouped).reshape(cell_count, C)

def reference(noisy_field, noise_draw, coarse_latent, particle_type, type_table, kv_weight, norm_gain, conv_weight, query_weight, mix_weight, out_weight):
    coarse_kv = coarse_keys(coarse_latent, particle_type, type_table, kv_weight)
    span_p, span_e = (noisy_field.shape[0], noisy_field.shape[1])
    stream = noisy_field.astype(jnp.float32).reshape(span_p, span_e, LAYERS, C)
    for block_idx in range(BLOCKS):
        normed = (stream * lax.rsqrt(lax.optimization_barrier(jnp.mean(stream * stream, axis=-1, keepdims=True)) + eps) * norm_gain[block_idx]).astype(jnp.bfloat16)
        wrapped = jnp.concatenate([normed[-1:], normed, normed[:1]], axis=0)
        padded = jnp.pad(wrapped, ((0, 0), (1, 1), (0, 0), (0, 0)))
        conv = convolve(padded, conv_weight[block_idx])
        activated = jax.nn.silu(conv).astype(jnp.bfloat16)
        flat = normed.reshape(-1, C)
        query = jnp.dot(flat, query_weight[block_idx], preferred_element_type=jnp.float32).astype(jnp.bfloat16)
        start = block_idx * 2 * C
        attended = attend(query, coarse_kv[:, start:start + C], coarse_kv[:, start + C:start + 2 * C])
        branch_one = jnp.dot(activated.reshape(-1, C), mix_weight[block_idx], preferred_element_type=jnp.float32)
        branch_two = jnp.dot(attended, out_weight[block_idx], preferred_element_type=jnp.float32)
        stream = stream + (branch_one + branch_two).reshape(stream.shape)
    flat_stream = stream.reshape(noisy_field.shape)
    denoised = 1.02 * (noisy_field.astype(jnp.float32) - 0.2 * flat_stream) + 0.3 * noise_draw.astype(jnp.float32)
    return denoised.astype(jnp.bfloat16)
```

```python
import math

import jax
import jax.numpy as jnp
from jax import lax
from jax.experimental import pallas as pl
from jax.experimental.pallas import tpu as pltpu
from jax.sharding import PartitionSpec as P

C = 96
LATENT = 512
TYPES = 8
HEADS = 2
BLOCKS = 2
LAYERS = 8
HDIM = 48
LANES = 128
EPS = 1e-06
SCORE_SCALE = 1.0 / math.sqrt(HDIM) * math.log2(math.e)
SAFE_SCORE = 96.0

F32 = jnp.float32
BF16 = jnp.bfloat16


def dot(a, b):
    return jnp.dot(a, b, preferred_element_type=F32)


def silu(x):
    return x / (1.0 + jnp.exp(-x))


def tokens_kernel(type_ref, latent_ref, table_ref, weight_ref, kv_ref):
    rows = latent_ref.shape[0]
    row = lax.broadcasted_iota(jnp.int32, (rows, TYPES), 0)
    column = lax.broadcasted_iota(jnp.int32, (rows, TYPES), 1)
    kind = jnp.zeros((rows, TYPES), jnp.int32)
    for i in range(rows):
        kind = jnp.where(row == i, type_ref[i], kind)
    picked = (kind == column).astype(F32).astype(BF16)
    embed = dot(picked, table_ref[...])
    hidden = jax.nn.silu(latent_ref[...].astype(F32) + embed).astype(BF16)
    kv_ref[...] = dot(hidden, weight_ref[...]).astype(BF16)


def local_tokens(coarse_latent, particle_type, type_table, kv_weight):
    vmem = pl.BlockSpec(memory_space=pltpu.VMEM)
    return pl.pallas_call(
        tokens_kernel,
        out_shape=jax.ShapeDtypeStruct((coarse_latent.shape[0], kv_weight.shape[1]), BF16),
        in_specs=[pl.BlockSpec(memory_space=pltpu.SMEM), vmem, vmem, vmem],
        out_specs=vmem,
        cost_estimate=pl.CostEstimate(flops=6_000_000, bytes_accessed=500_000, transcendentals=8192),
        name="tokens",
    )(particle_type, coarse_latent, type_table, kv_weight)


def phi_index(x, y, z, core):
    return ((x * 2 + y) * 8 + z) * 2 + core


YZ_GROUPS = [
    [phi_index(x, y, z, c) for y in range(2) for z in range(8)] for x in range(4) for c in range(2)
]
X_GROUPS = [
    [phi_index(x, y, z, c) for x in range(4)] for y in range(2) for z in range(8) for c in range(2)
]


def spread(rows, groups):
    count = len(groups[0])
    copies = jnp.broadcast_to(rows[None], (count,) + rows.shape)
    return lax.all_to_all(
        copies, "phi", 0, 0, tiled=True, axis_index_groups=groups
    ).reshape(-1, rows.shape[-1])


def gather_tokens(kv):
    count = lax.axis_size("phi")
    if count != 128:
        return lax.all_gather(kv, "phi", axis=0, tiled=True)
    kv = spread(kv, YZ_GROUPS)
    kv = spread(kv, X_GROUPS)
    other = lax.ppermute(kv, "phi", [(i, i ^ 1) for i in range(count)])
    return jnp.concatenate([kv, other], axis=0)


def halo(field):
    count = lax.axis_size("phi")
    up = [(i, (i + 1) % count) for i in range(count)]
    down = [((i + 1) % count, i) for i in range(count)]
    top = lax.ppermute(field[-2:], "phi", up)
    bottom = lax.ppermute(field[:2], "phi", down)
    bands = lax.axis_size("eta")
    right = [(i, i + 1) for i in range(bands - 1)]
    left = [(i + 1, i) for i in range(bands - 1)]
    west = jnp.concatenate([top[:, -2:], field[:, -2:], bottom[:, -2:]], axis=0)
    east = jnp.concatenate([top[:, :2], field[:, :2], bottom[:, :2]], axis=0)
    return top, bottom, lax.ppermute(west, "eta", right), lax.ppermute(east, "eta", left)


def normalized(x, gain):
    mean = jnp.sum(x * x, axis=-1, keepdims=True) * (1.0 / C)
    return (x * lax.rsqrt(mean + EPS) * gain).astype(BF16)


def conv_branch(taps, row, start, length, weight_ref, mix_ref):
    conv = jnp.zeros((length, C), F32)
    for di in range(3):
        for dj in range(3):
            shifted = taps[row + di, start + 8 * dj : start + 8 * dj + length, :]
            conv = conv + dot(shifted, weight_ref[3 * di + dj])
    return dot(silu(conv).astype(BF16), mix_ref[...])


def front_kernel(
    field_ref, top_ref, bottom_ref, west_ref, east_ref, gain_ref, conv_ref, query_ref, mix_ref,
    acc_ref, q_ref, cells, taps,
):
    span_p, span_e = field_ref.shape[0], field_ref.shape[1]

    def put(row, start, piece):
        count = piece.shape[0]
        zeros = jnp.zeros((count, LANES - C), F32)
        for layer in range(LAYERS):
            part = piece[:, layer * C : (layer + 1) * C]
            cells[row, pl.ds(start * LAYERS + layer, count, stride=LAYERS), :] = jnp.concatenate(
                [part, zeros], axis=1
            )

    for row in range(span_p + 4):
        if row < 2:
            middle = top_ref[row]
        elif row < span_p + 2:
            middle = field_ref[row - 2]
        else:
            middle = bottom_ref[row - span_p - 2]
        put(row, 2, middle.astype(F32))
        put(row, 0, west_ref[row].astype(F32))
        put(row, span_e + 2, east_ref[row].astype(F32))
    for row in range(span_p + 4):
        taps[row] = normalized(cells[row][:, :C], gain_ref[...])
    length = (span_e + 2) * LAYERS
    for row in range(span_p + 2):
        branch = conv_branch(taps, row, 0, length, conv_ref, mix_ref)
        acc_ref[row] = cells[row + 1, 8 : 8 + length, :C] + branch
        q = dot(taps[row + 1, 8 : 8 + length, :], query_ref[...]) * SCORE_SCALE
        q_ref[row] = q.astype(BF16)


def front(field, top, bottom, west, east, gain, conv_weight, query_weight, mix_weight):
    span_p, span_e = field.shape[0], field.shape[1]
    vmem = pl.BlockSpec(memory_space=pltpu.VMEM)
    rows, width = span_p + 2, (span_e + 2) * LAYERS
    return pl.pallas_call(
        front_kernel,
        out_shape=[
            jax.ShapeDtypeStruct((rows, width, C), F32),
            jax.ShapeDtypeStruct((rows, width, C), BF16),
        ],
        in_specs=[vmem] * 9,
        out_specs=[vmem] * 2,
        scratch_shapes=[
            pltpu.VMEM((span_p + 4, (span_e + 4) * LAYERS, LANES), F32),
            pltpu.VMEM((span_p + 4, (span_e + 4) * LAYERS, C), BF16),
        ],
        compiler_params=pltpu.CompilerParams(vmem_limit_bytes=40 * 1024 * 1024),
        cost_estimate=pl.CostEstimate(flops=6_000_000_000, bytes_accessed=5_000_000, transcendentals=400_000),
        name="front",
    )(field, top, bottom, west, east, gain, conv_weight, query_weight, mix_weight)


def prepare_tokens(kv_ref, block, keys, values):
    start = 2 * C * block
    keys[block] = jnp.transpose(kv_ref[:, start : start + C])
    value = kv_ref[:, start + C : start + 2 * C]
    value = jnp.concatenate([value, jnp.zeros((value.shape[0], LANES - C), BF16)], axis=1)
    lane = lax.broadcasted_iota(jnp.int32, value.shape, 1)
    for head in range(HEADS):
        mine = (lane >= head * HDIM) & (lane < (head + 1) * HDIM)
        one = (lane == C).astype(BF16)
        values[block, head] = jnp.where(mine, value, one)


def largest_key(keys, block, head):
    key = keys[block, head * HDIM : (head + 1) * HDIM, :].astype(F32)
    return jnp.max(jnp.sum(key * key, axis=0, keepdims=True))


def attend(q, block, keys, values, safe):
    result = None
    lane = lax.broadcasted_iota(jnp.int32, (q.shape[0], C), 1)
    for head in range(HEADS):
        span = slice(head * HDIM, (head + 1) * HDIM)
        scores = dot(q[:, span], keys[block, span, :])
        if not safe:
            scores = scores - jnp.max(scores, axis=-1, keepdims=True)
        probs = jnp.exp2(scores).astype(BF16)
        out = dot(probs, values[block, head])
        out = out[:, :C] * (1.0 / out[:, C : C + 1])
        result = out if head == 0 else jnp.where(lane < HDIM, result, out)
    return result.astype(BF16)


def within(q, biggest):
    q = q.astype(F32)
    square = q * q
    lane = lax.broadcasted_iota(jnp.int32, q.shape, 1)
    first = jnp.sum(jnp.where(lane < HDIM, square, 0.0), axis=-1, keepdims=True)
    second = jnp.sum(jnp.where(lane < HDIM, 0.0, square), axis=-1, keepdims=True)
    worst = jnp.maximum(jnp.max(first) * biggest[0], jnp.max(second) * biggest[1])
    return worst <= SAFE_SCORE * SAFE_SCORE


def back_kernel(
    edge_ref, acc_ref, q_ref, kv_ref, field_ref, noise_ref, gain_ref, conv_ref, query_ref, mix_ref,
    out_ref, result_ref, keys, values, attended, stream, taps, flat,
):
    span_p, span_e = field_ref.shape[0], field_ref.shape[1]
    width, inner = (span_e + 2) * LAYERS, span_e * LAYERS
    for block in range(BLOCKS):
        prepare_tokens(kv_ref, block, keys, values)
    biggest = [[largest_key(keys, b, h) for h in range(HEADS)] for b in range(BLOCKS)]

    def attend_rows(q, block, rows):
        fine = within(q, biggest[block])

        @pl.when(fine)
        def _():
            attended[0:rows, :] = attend(q, block, keys, values, True)

        @pl.when(jnp.logical_not(fine))
        def _():
            attended[0:rows, :] = attend(q, block, keys, values, False)

    @pl.loop(0, span_p + 2)
    def _(row):
        attend_rows(q_ref[row], 0, width)
        new = acc_ref[row] + dot(attended[...], out_ref[0])
        stream[row] = new
        place = lax.broadcasted_iota(jnp.int32, new.shape, 0)
        outside = ((place < LAYERS) & (edge_ref[0] == 1)) | (
            (place >= width - LAYERS) & (edge_ref[1] == 1)
        )
        taps[row] = normalized(jnp.where(outside, 0.0, new), gain_ref[...])

    @pl.loop(0, span_p)
    def _(row):
        branch = conv_branch(taps, row, 0, inner, conv_ref, mix_ref)
        q = dot(taps[row + 1, LAYERS : LAYERS + inner, :], query_ref[...]) * SCORE_SCALE
        attend_rows(q.astype(BF16), 1, inner)
        new = stream[row + 1, LAYERS : LAYERS + inner, :] + branch
        new = new + dot(attended[0:inner, :], out_ref[1])
        flat[...] = jnp.concatenate([new, jnp.zeros((inner, LANES - C), F32)], axis=1)
        for layer in range(LAYERS):
            last = flat[pl.ds(layer, span_e, stride=LAYERS), :][:, :C]
            span = slice(layer * C, (layer + 1) * C)
            field = field_ref[row, :, span].astype(F32)
            noise = noise_ref[row, :, span].astype(F32)
            result_ref[row, :, span] = (1.02 * (field - 0.2 * last) + 0.3 * noise).astype(BF16)


def back(edges, acc, q, kv, field, noise, gain, conv_weight, query_weight, mix_weight, out_weight):
    span_p, span_e = field.shape[0], field.shape[1]
    vmem = pl.BlockSpec(memory_space=pltpu.VMEM)
    tokens = kv.shape[0]
    rows, width = span_p + 2, (span_e + 2) * LAYERS
    return pl.pallas_call(
        back_kernel,
        out_shape=jax.ShapeDtypeStruct(field.shape, BF16),
        in_specs=[pl.BlockSpec(memory_space=pltpu.SMEM)] + [vmem] * 10,
        out_specs=vmem,
        scratch_shapes=[
            pltpu.VMEM((BLOCKS, C, tokens), BF16),
            pltpu.VMEM((BLOCKS, HEADS, tokens, LANES), BF16),
            pltpu.VMEM((width, C), BF16),
            pltpu.VMEM((rows, width, C), F32),
            pltpu.VMEM((rows, width, C), BF16),
            pltpu.VMEM((span_e * LAYERS, LANES), F32),
        ],
        compiler_params=pltpu.CompilerParams(vmem_limit_bytes=52 * 1024 * 1024),
        cost_estimate=pl.CostEstimate(
            flops=20_000_000_000, bytes_accessed=6_000_000, transcendentals=21_000_000
        ),
        name="back",
    )(edges, acc, q, kv, field, noise, gain, conv_weight, query_weight, mix_weight, out_weight)


def body(
    noisy_field,
    noise_draw,
    coarse_latent,
    particle_type,
    type_table,
    kv_weight,
    norm_gain,
    conv_weight,
    query_weight,
    mix_weight,
    out_weight,
):
    top, bottom, west, east = halo(noisy_field)
    local = local_tokens(coarse_latent, particle_type, type_table, kv_weight)
    kv = gather_tokens(local)
    acc, q = front(
        noisy_field, top, bottom, west, east, norm_gain[0:1], conv_weight[0], query_weight[0],
        mix_weight[0],
    )
    band = lax.axis_index("eta")
    edges = jnp.stack([band == 0, band == lax.axis_size("eta") - 1]).astype(jnp.int32)
    return back(
        edges, acc, q, kv, noisy_field, noise_draw, norm_gain[1:2], conv_weight[1],
        query_weight[1], mix_weight[1], out_weight,
    )


def solution(mesh):
    in_specs = (
        P("phi", "eta", None),
        P("phi", "eta", None),
        P("phi", None),
        P("phi"),
        P(),
        P(),
        P(),
        P(),
        P(),
        P(),
        P(),
    )
    out_specs = P("phi", "eta", None)
    return jax.shard_map(body, mesh=mesh, in_specs=in_specs, out_specs=out_specs, check_vma=False)
```

```python
import math

import jax
import jax.numpy as jnp
from jax import lax
from jax.experimental import pallas as pl
from jax.experimental.pallas import tpu as pltpu
from jax.sharding import PartitionSpec as P

C = 96
LATENT = 512
TYPES = 8
HEADS = 2
BLOCKS = 2
LAYERS = 8
HDIM = 48
LANES = 128
EPS = 1e-06
SCORE_SCALE = 1.0 / math.sqrt(HDIM) * math.log2(math.e)
SAFE_SCORE = 96.0
TILE = 1024

F32 = jnp.float32
BF16 = jnp.bfloat16


def dot(a, b):
    return jnp.dot(a, b, preferred_element_type=F32)


def silu(x):
    return 0.5 * x * (1.0 + jnp.tanh(0.5 * x))


def tokens_kernel(type_ref, latent_ref, table_ref, weight_ref, kv_ref):
    rows = latent_ref.shape[0]
    row = lax.broadcasted_iota(jnp.int32, (rows, TYPES), 0)
    column = lax.broadcasted_iota(jnp.int32, (rows, TYPES), 1)
    kind = jnp.zeros((rows, TYPES), jnp.int32)
    for i in range(rows):
        kind = jnp.where(row == i, type_ref[i], kind)
    picked = (kind == column).astype(F32).astype(BF16)
    embed = dot(picked, table_ref[...])
    hidden = jax.nn.silu(latent_ref[...].astype(F32) + embed).astype(BF16)
    kv = dot(hidden, weight_ref[...]).astype(BF16)
    for i in range(kv_ref.shape[0]):
        kv_ref[i] = kv


def local_tokens(coarse_latent, particle_type, type_table, kv_weight, copies):
    vmem = pl.BlockSpec(memory_space=pltpu.VMEM)
    return pl.pallas_call(
        tokens_kernel,
        out_shape=jax.ShapeDtypeStruct(
            (copies, coarse_latent.shape[0], kv_weight.shape[1]), BF16
        ),
        in_specs=[pl.BlockSpec(memory_space=pltpu.SMEM), vmem, vmem, vmem],
        out_specs=vmem,
        cost_estimate=pl.CostEstimate(flops=6_000_000, bytes_accessed=700_000, transcendentals=8192),
        name="tokens",
    )(particle_type, coarse_latent, type_table, kv_weight)


def phi_index(x, y, z, core):
    return ((x * 2 + y) * 8 + z) * 2 + core


YZ_GROUPS = [
    [phi_index(x, y, z, c) for y in range(2) for z in range(8)] for x in range(4) for c in range(2)
]
X_GROUPS = [
    [phi_index(x, y, z, c) for x in range(4)] for y in range(2) for z in range(8) for c in range(2)
]


def exchange(copies, groups):
    rows = lax.all_to_all(copies, "phi", 0, 0, tiled=True, axis_index_groups=groups)
    return rows.reshape(-1, rows.shape[-1])


def halo_phi(field):
    count = lax.axis_size("phi")
    up = [(i, (i + 1) % count) for i in range(count)]
    down = [((i + 1) % count, i) for i in range(count)]
    return lax.ppermute(field[-2:], "phi", up), lax.ppermute(field[:2], "phi", down)


def halo_eta(field, top, bottom):
    bands = lax.axis_size("eta")
    right = [(i, i + 1) for i in range(bands - 1)]
    left = [(i + 1, i) for i in range(bands - 1)]
    west = jnp.concatenate([top[:, -2:], field[:, -2:], bottom[:, -2:]], axis=0)
    east = jnp.concatenate([top[:, :2], field[:, :2], bottom[:, :2]], axis=0)
    return lax.ppermute(west, "eta", right), lax.ppermute(east, "eta", left)


def normalized(x, gain):
    mean = jnp.sum(x * x, axis=-1, keepdims=True) * (1.0 / C)
    return x * lax.rsqrt(mean + EPS) * gain


def widened(x):
    return jnp.concatenate([x, jnp.zeros((x.shape[0], LANES - C), x.dtype)], axis=1)


def keep_taps(normed, row, outer, centre):
    outer[row] = normed.astype(BF16)
    centre[row] = normed[LAYERS:-LAYERS].astype(BF16)


def pack_weight(weight_ref, block, packed):
    packed[...] = jnp.zeros_like(packed)
    for tap in range(9):
        packed[tap * LANES : tap * LANES + C, :] = weight_ref[block, tap]


def conv_branch(outer, centre, row, length, packed, mix):
    taps = []
    for di in range(3):
        taps.append(outer[row + di, 0:length, :])
        taps.append(centre[row + di, 0:length, :])
        taps.append(outer[row + di, 2 * LAYERS : 2 * LAYERS + length, :])
    conv = dot(jnp.concatenate(taps, axis=1), packed[...])
    return dot(silu(conv).astype(BF16), mix)


def front_kernel(
    field_ref, top_ref, bottom_ref, west_ref, east_ref, gain_ref, conv_ref, query_ref, mix_ref,
    acc_ref, q_ref, done_ref, cells, outer, centre, packed, acc, queries, sems,
):
    span_p, span_e = field_ref.shape[0], field_ref.shape[1]
    length = (span_e + 2) * LAYERS
    gain = widened(gain_ref[0:1, :])
    pack_weight(conv_ref, 0, packed)

    def put(row, start, piece):
        count = piece.shape[0]
        for layer in range(LAYERS):
            part = piece[:, layer * C : (layer + 1) * C]
            cells[row, pl.ds(start * LAYERS + layer, count, stride=LAYERS), :] = widened(part)

    for row in range(span_p + 4):
        if row < 2:
            middle = top_ref[row]
        elif row < span_p + 2:
            middle = field_ref[row - 2]
        else:
            middle = bottom_ref[row - span_p - 2]
        put(row, 2, middle.astype(F32))
        put(row, 0, west_ref[row].astype(F32))
        put(row, span_e + 2, east_ref[row].astype(F32))
        keep_taps(normalized(cells[row], gain), row, outer, centre)
    copies = []
    for row in range(span_p + 2):
        branch = conv_branch(outer, centre, row, length, packed, mix_ref[0])
        acc[row] = cells[row + 1, LAYERS : LAYERS + length, :][:, :C] + branch
        q = dot(centre[row + 1][:, :C], query_ref[0])
        span = slice(row * length, (row + 1) * length)
        queries[span, :] = q.astype(BF16)
        copies.append(pltpu.make_async_copy(acc.at[row], acc_ref.at[row], sems.at[0, row]))
        copies.append(pltpu.make_async_copy(queries.at[span], q_ref.at[span], sems.at[1, row]))
        copies[-2].start()
        copies[-1].start()
    for copy in copies:
        copy.wait()
    done_ref[...] = jnp.zeros_like(done_ref)


def front(field, top, bottom, west, east, gain, conv_weight, query_weight, mix_weight):
    span_p, span_e = field.shape[0], field.shape[1]
    vmem = pl.BlockSpec(memory_space=pltpu.VMEM)
    rows, width = span_p + 2, (span_e + 2) * LAYERS
    return pl.pallas_call(
        front_kernel,
        out_shape=[
            jax.ShapeDtypeStruct((rows, width, C), F32),
            jax.ShapeDtypeStruct((rows * width, C), BF16),
            jax.ShapeDtypeStruct((8, LANES), BF16),
        ],
        in_specs=[vmem] * 9,
        out_specs=[pl.BlockSpec(memory_space=pltpu.HBM)] * 2 + [vmem],
        scratch_shapes=[
            pltpu.VMEM((rows + 2, width + 2 * LAYERS, LANES), F32),
            pltpu.VMEM((rows + 2, width + 2 * LAYERS, LANES), BF16),
            pltpu.VMEM((rows + 2, width, LANES), BF16),
            pltpu.VMEM((9 * LANES, C), BF16),
            pltpu.VMEM((rows, width, C), F32),
            pltpu.VMEM((rows * width, C), BF16),
            pltpu.SemaphoreType.DMA((2, rows)),
        ],
        compiler_params=pltpu.CompilerParams(vmem_limit_bytes=60 * 1024 * 1024),
        cost_estimate=pl.CostEstimate(
            flops=6_000_000_000, bytes_accessed=5_000_000, transcendentals=400_000
        ),
        name="front",
    )(field, top, bottom, west, east, gain, conv_weight, query_weight, mix_weight)


def prepare_tokens(kv_refs, keys, values):
    tokens = kv_refs[0].shape[0]
    largest = [[0.0] * HEADS for _ in range(BLOCKS)]
    pad = values.shape[2] - HDIM
    ones = (lax.broadcasted_iota(jnp.int32, (pad, tokens), 0) == 0).astype(F32).astype(BF16)
    for part, kv_ref in enumerate(kv_refs):
        span = slice(part * tokens, (part + 1) * tokens)
        turned = jnp.transpose(kv_ref[...])
        for block in range(BLOCKS):
            start = 2 * C * block
            keys[block, span, :] = kv_ref[:, start : start + C]
            for head in range(HEADS):
                low = start + head * HDIM
                key = turned[low : low + HDIM].astype(F32)
                longest = jnp.max(jnp.sum(key * key, axis=0, keepdims=True))
                largest[block][head] = jnp.maximum(largest[block][head], longest)
                values[block, head, 0:HDIM, span] = turned[low + C : low + C + HDIM]
                values[block, head, HDIM : HDIM + pad, span] = ones
    return largest


def attend(q, keys, values, safe):
    head_row = lax.broadcasted_iota(jnp.int32, q.shape, 0)
    results = []
    for head in range(HEADS):
        mine = (head_row >= head * HDIM) & (head_row < (head + 1) * HDIM)
        scores = dot(keys[...], jnp.where(mine, q, jnp.zeros_like(q)))
        if not safe:
            scores = scores - jnp.max(scores, axis=0, keepdims=True)
        probs = jnp.exp2(scores * SCORE_SCALE).astype(BF16)
        out = dot(values[head], probs)
        results.append(out[:HDIM] * (1.0 / out[HDIM : HDIM + 1]))
    return jnp.concatenate(results, axis=0).astype(BF16)


def within(q, largest):
    square = q.astype(F32)
    square = square * square
    worst = [
        jnp.max(jnp.sum(square[h * HDIM : (h + 1) * HDIM], axis=0, keepdims=True)) * largest[h]
        for h in range(HEADS)
    ]
    return jnp.maximum(worst[0], worst[1]) <= (SAFE_SCORE / SCORE_SCALE) ** 2


def back_kernel(
    edge_ref, _, acc_ref, q_ref, kv_ref, other_ref, field_in, noise_in, gain_ref, conv_ref,
    query_ref, mix_ref, out_ref, result_ref, keys, values, attended, second, stream, outer, centre,
    packed, flat, acc, queries, field_ref, noise_ref, sems,
):
    span_p, span_e = field_ref.shape[0], field_ref.shape[1]
    width, inner = (span_e + 2) * LAYERS, span_e * LAYERS
    q_copy = pltpu.make_async_copy(q_ref, queries, sems.at[0])
    acc_copy = pltpu.make_async_copy(acc_ref, acc, sems.at[1])
    late = [
        pltpu.make_async_copy(field_in, field_ref, sems.at[2]),
        pltpu.make_async_copy(noise_in, noise_ref, sems.at[3]),
    ]
    for copy in [q_copy, acc_copy] + late:
        copy.start()
    gain = widened(gain_ref[1:2, :])
    largest = prepare_tokens([kv_ref, other_ref], keys, values)
    pack_weight(conv_ref, 1, packed)

    def attend_rows(source, block, start, rows):
        q = jnp.transpose(source[pl.ds(start, rows), :])
        fine = within(q, largest[block])

        def go(safe):
            found = attend(q, keys.at[block], values.at[block], safe)
            attended[pl.ds(start, rows), :] = jnp.transpose(found)

        pl.when(fine)(lambda: go(True))
        pl.when(jnp.logical_not(fine))(lambda: go(False))

    def attend_all(source, block, count):
        tiles = count // TILE

        @pl.loop(0, tiles)
        def _(tile):
            attend_rows(source, block, pl.multiple_of(tile * TILE, TILE), TILE)

        rest = count - tiles * TILE
        if rest:
            rest = -(-rest // LANES) * LANES
            attend_rows(source, block, count - rest, rest)

    q_copy.wait()
    attend_all(queries, 0, (span_p + 2) * width)
    acc_copy.wait()
    for row in range(span_p + 2):
        branch = dot(attended[row * width : (row + 1) * width, :], out_ref[0])
        new = acc[row] + branch
        if 0 < row < span_p + 1:
            stream[row - 1] = new[LAYERS:-LAYERS]
        place = lax.broadcasted_iota(jnp.int32, new.shape, 0)
        outside = ((place < LAYERS) & (edge_ref[0] == 1)) | (
            (place >= width - LAYERS) & (edge_ref[1] == 1)
        )
        normed = normalized(widened(jnp.where(outside, 0.0, new)), gain)
        keep_taps(normed, row, outer, centre)
        if 0 < row < span_p + 1:
            q = dot(centre[row][:, :C], query_ref[1])
            second[(row - 1) * inner : row * inner, :] = q.astype(BF16)

    attend_all(second, 1, span_p * inner)
    for copy in late:
        copy.wait()
    for row in range(span_p):
        branch = conv_branch(outer, centre, row, inner, packed, mix_ref[1])
        new = stream[row] + branch + dot(attended[row * inner : (row + 1) * inner, :], out_ref[1])
        flat[...] = widened(new)
        for layer in range(LAYERS):
            last = flat[pl.ds(layer, span_e, stride=LAYERS), :][:, :C]
            span = slice(layer * C, (layer + 1) * C)
            field = field_ref[row, :, span].astype(F32)
            noise = noise_ref[row, :, span].astype(F32)
            result_ref[row, :, span] = (1.02 * (field - 0.2 * last) + 0.3 * noise).astype(BF16)


def back(edges, done, acc, q, kv, other, field, noise, gain, conv_weight, query_weight, mix_weight, out_weight):
    span_p, span_e = field.shape[0], field.shape[1]
    vmem = pl.BlockSpec(memory_space=pltpu.VMEM)
    tokens = kv.shape[0] + other.shape[0]
    rows, width, inner = span_p + 2, (span_e + 2) * LAYERS, span_e * LAYERS
    return pl.pallas_call(
        back_kernel,
        out_shape=jax.ShapeDtypeStruct(field.shape, BF16),
        in_specs=[pl.BlockSpec(memory_space=pltpu.SMEM), pl.BlockSpec(memory_space=pl.ANY)]
        + [pl.BlockSpec(memory_space=pltpu.HBM)] * 2
        + [vmem] * 2
        + [pl.BlockSpec(memory_space=pl.ANY)] * 2
        + [vmem] * 5,
        out_specs=vmem,
        scratch_shapes=[
            pltpu.VMEM((BLOCKS, tokens, C), BF16),
            pltpu.VMEM((BLOCKS, HEADS, 64, tokens), BF16),
            pltpu.VMEM((rows * width, C), BF16),
            pltpu.VMEM((span_p * inner, C), BF16),
            pltpu.VMEM((span_p, inner, C), F32),
            pltpu.VMEM((rows, width, LANES), BF16),
            pltpu.VMEM((rows, inner, LANES), BF16),
            pltpu.VMEM((9 * LANES, C), BF16),
            pltpu.VMEM((inner, LANES), F32),
            pltpu.VMEM((rows, width, C), F32),
            pltpu.VMEM((rows * width, C), BF16),
            pltpu.VMEM(field.shape, BF16),
            pltpu.VMEM(field.shape, BF16),
            pltpu.SemaphoreType.DMA((4,)),
        ],
        compiler_params=pltpu.CompilerParams(vmem_limit_bytes=60 * 1024 * 1024),
        cost_estimate=pl.CostEstimate(
            flops=20_000_000_000, bytes_accessed=6_000_000, transcendentals=21_000_000
        ),
        name="back",
    )(edges, done, acc, q, kv, other, field, noise, gain, conv_weight, query_weight, mix_weight, out_weight)


def tokens_and_front(
    coarse_latent, particle_type, type_table, kv_weight, field, gain, conv_weight, query_weight,
    mix_weight,
):
    local = local_tokens(coarse_latent, particle_type, type_table, kv_weight, len(YZ_GROUPS[0]))
    top, bottom = halo_phi(field)
    west, east = halo_eta(field, top, bottom)
    kv = exchange(local, YZ_GROUPS)
    kv, west, east = lax.optimization_barrier((kv, west, east))
    acc, q, done = front(
        field, top, bottom, west, east, gain, conv_weight, query_weight, mix_weight
    )
    copies = jnp.broadcast_to(kv[None], (len(X_GROUPS[0]),) + kv.shape)
    kv = exchange(copies, X_GROUPS)
    kv, done = lax.optimization_barrier((kv, done))
    other = lax.ppermute(kv, "phi", [(i, i ^ 1) for i in range(lax.axis_size("phi"))])
    return kv, other, acc, q, done


def body(
    noisy_field,
    noise_draw,
    coarse_latent,
    particle_type,
    type_table,
    kv_weight,
    norm_gain,
    conv_weight,
    query_weight,
    mix_weight,
    out_weight,
):
    kv, other, acc, q, done = tokens_and_front(
        coarse_latent, particle_type, type_table, kv_weight, noisy_field, norm_gain, conv_weight,
        query_weight, mix_weight,
    )
    band = lax.axis_index("eta")
    edges = jnp.stack([band == 0, band == lax.axis_size("eta") - 1]).astype(jnp.int32)
    return back(
        edges, done, acc, q, kv, other, noisy_field, noise_draw, norm_gain, conv_weight, query_weight,
        mix_weight, out_weight,
    )


def solution(mesh):
    in_specs = (
        P("phi", "eta", None),
        P("phi", "eta", None),
        P("phi", None),
        P("phi"),
        P(),
        P(),
        P(),
        P(),
        P(),
        P(),
        P(),
    )
    out_specs = P("phi", "eta", None)
    return jax.shard_map(body, mesh=mesh, in_specs=in_specs, out_specs=out_specs, check_vma=False)
```

```python
import math

import jax
import jax.numpy as jnp
from jax import lax
from jax.experimental import pallas as pl
from jax.experimental.pallas import tpu as pltpu
from jax.sharding import PartitionSpec as P

C = 96
LATENT = 512
TYPES = 8
HEADS = 2
BLOCKS = 2
LAYERS = 8
HDIM = 48
LANES = 128
EPS = 1e-06
SCORE_SCALE = 1.0 / math.sqrt(HDIM) * math.log2(math.e)
SAFE_SCORE = 96.0
TILES = (1024, 1024)

F32 = jnp.float32
BF16 = jnp.bfloat16


def dot(a, b):
    return jnp.dot(a, b, preferred_element_type=F32)


def silu(x):
    return 0.5 * x * (1.0 + jnp.tanh(0.5 * x))


def tokens_kernel(type_ref, latent_ref, table_ref, weight_ref, kv_ref):
    rows = latent_ref.shape[0]
    row = lax.broadcasted_iota(jnp.int32, (rows, TYPES), 0)
    column = lax.broadcasted_iota(jnp.int32, (rows, TYPES), 1)
    kind = jnp.zeros((rows, TYPES), jnp.int32)
    for i in range(rows):
        kind = jnp.where(row == i, type_ref[i], kind)
    picked = (kind == column).astype(F32).astype(BF16)
    embed = dot(picked, table_ref[...])
    hidden = jax.nn.silu(latent_ref[...].astype(F32) + embed).astype(BF16)
    kv = dot(hidden, weight_ref[...]).astype(BF16)
    for i in range(kv_ref.shape[0]):
        kv_ref[i] = kv


def local_tokens(coarse_latent, particle_type, type_table, kv_weight, copies):
    vmem = pl.BlockSpec(memory_space=pltpu.VMEM)
    return pl.pallas_call(
        tokens_kernel,
        out_shape=jax.ShapeDtypeStruct(
            (copies, coarse_latent.shape[0], kv_weight.shape[1]), BF16
        ),
        in_specs=[pl.BlockSpec(memory_space=pltpu.SMEM), vmem, vmem, vmem],
        out_specs=vmem,
        cost_estimate=pl.CostEstimate(flops=6_000_000, bytes_accessed=700_000, transcendentals=8192),
        name="tokens",
    )(particle_type, coarse_latent, type_table, kv_weight)


def phi_index(x, y, z, core):
    return ((x * 2 + y) * 8 + z) * 2 + core


YZ_GROUPS = [
    [phi_index(x, y, z, c) for y in range(2) for z in range(8)] for x in range(4) for c in range(2)
]
X_GROUPS = [
    [phi_index(x, y, z, c) for x in range(4)] for y in range(2) for z in range(8) for c in range(2)
]


def exchange(copies, groups):
    rows = lax.all_to_all(copies, "phi", 0, 0, tiled=True, axis_index_groups=groups)
    return rows.reshape(-1, rows.shape[-1])


def halo_phi(field):
    count = lax.axis_size("phi")
    up = [(i, (i + 1) % count) for i in range(count)]
    down = [((i + 1) % count, i) for i in range(count)]
    return lax.ppermute(field[-2:], "phi", up), lax.ppermute(field[:2], "phi", down)


def halo_eta(field, top, bottom):
    bands = lax.axis_size("eta")
    right = [(i, i + 1) for i in range(bands - 1)]
    left = [(i + 1, i) for i in range(bands - 1)]
    west = jnp.concatenate([top[:, -2:], field[:, -2:], bottom[:, -2:]], axis=0)
    east = jnp.concatenate([top[:, :2], field[:, :2], bottom[:, :2]], axis=0)
    return lax.ppermute(west, "eta", right), lax.ppermute(east, "eta", left)


def normalized(x, gain):
    mean = jnp.sum(x * x, axis=-1, keepdims=True) * (1.0 / C)
    return x * lax.rsqrt(mean + EPS) * gain


def widened(x):
    return jnp.concatenate([x, jnp.zeros((x.shape[0], LANES - C), x.dtype)], axis=1)


def keep_taps(normed, row, outer, centre):
    outer[row] = normed.astype(BF16)
    centre[row] = normed[LAYERS:-LAYERS].astype(BF16)


def pack_weight(weight_ref, block, packed):
    packed[...] = jnp.zeros_like(packed)
    for tap in range(9):
        packed[tap * LANES : tap * LANES + C, :] = weight_ref[block, tap]


def conv_branch(outer, centre, row, length, packed, mix):
    taps = []
    for di in range(3):
        taps.append(outer[row + di, 0:length, :])
        taps.append(centre[row + di, 0:length, :])
        taps.append(outer[row + di, 2 * LAYERS : 2 * LAYERS + length, :])
    conv = dot(jnp.concatenate(taps, axis=1), packed[...])
    return dot(silu(conv).astype(BF16), mix)


def front_kernel(
    _, field_ref, top_ref, bottom_ref, west_ref, east_ref, gain_ref, conv_ref, query_ref, mix_ref,
    acc_ref, q_ref, done_ref, cells, outer, centre, packed, acc, queries, sems,
):
    span_p, span_e = field_ref.shape[0], field_ref.shape[1]
    length = (span_e + 2) * LAYERS
    gain = widened(gain_ref[0:1, :])
    pack_weight(conv_ref, 0, packed)

    def put(row, start, piece):
        count = piece.shape[0]
        for layer in range(LAYERS):
            part = piece[:, layer * C : (layer + 1) * C]
            cells[row, pl.ds(start * LAYERS + layer, count, stride=LAYERS), :] = widened(part)

    for row in range(span_p + 4):
        if row < 2:
            middle = top_ref[row]
        elif row < span_p + 2:
            middle = field_ref[row - 2]
        else:
            middle = bottom_ref[row - span_p - 2]
        put(row, 2, middle.astype(F32))
        put(row, 0, west_ref[row].astype(F32))
        put(row, span_e + 2, east_ref[row].astype(F32))
        keep_taps(normalized(cells[row], gain), row, outer, centre)
    copies = []
    for row in range(span_p + 2):
        branch = conv_branch(outer, centre, row, length, packed, mix_ref[0])
        acc[row] = cells[row + 1, LAYERS : LAYERS + length, :][:, :C] + branch
        q = dot(centre[row + 1][:, :C], query_ref[0])
        span = slice(row * length, (row + 1) * length)
        queries[span, :] = q.astype(BF16)
        copies.append(pltpu.make_async_copy(acc.at[row], acc_ref.at[row], sems.at[0, row]))
        copies.append(pltpu.make_async_copy(queries.at[span], q_ref.at[span], sems.at[1, row]))
        copies[-2].start()
        copies[-1].start()
    for copy in copies:
        copy.wait()
    done_ref[...] = jnp.zeros_like(done_ref)


def front(edges, field, top, bottom, west, east, gain, conv_weight, query_weight, mix_weight):
    span_p, span_e = field.shape[0], field.shape[1]
    vmem = pl.BlockSpec(memory_space=pltpu.VMEM)
    rows, width = span_p + 2, (span_e + 2) * LAYERS
    return pl.pallas_call(
        front_kernel,
        out_shape=[
            jax.ShapeDtypeStruct((rows, width, C), F32),
            jax.ShapeDtypeStruct((rows * width, C), BF16),
            jax.ShapeDtypeStruct((8, LANES), BF16),
        ],
        in_specs=[pl.BlockSpec(memory_space=pltpu.SMEM)] + [vmem] * 9,
        out_specs=[pl.BlockSpec(memory_space=pltpu.HBM)] * 2 + [vmem],
        scratch_shapes=[
            pltpu.VMEM((rows + 2, width + 2 * LAYERS, LANES), F32),
            pltpu.VMEM((rows + 2, width + 2 * LAYERS, LANES), BF16),
            pltpu.VMEM((rows + 2, width, LANES), BF16),
            pltpu.VMEM((9 * LANES, C), BF16),
            pltpu.VMEM((rows, width, C), F32),
            pltpu.VMEM((rows * width, C), BF16),
            pltpu.SemaphoreType.DMA((2, rows)),
        ],
        compiler_params=pltpu.CompilerParams(vmem_limit_bytes=60 * 1024 * 1024),
        cost_estimate=pl.CostEstimate(
            flops=6_000_000_000, bytes_accessed=5_000_000, transcendentals=400_000
        ),
        name="front",
    )(edges, field, top, bottom, west, east, gain, conv_weight, query_weight, mix_weight)


def prepare_tokens(kv_refs, keys, values):
    tokens = kv_refs[0].shape[0]
    largest = [[0.0] * HEADS for _ in range(BLOCKS)]
    pad = values.shape[2] - HDIM
    ones = (lax.broadcasted_iota(jnp.int32, (pad, tokens), 0) == 0).astype(F32).astype(BF16)
    for part, kv_ref in enumerate(kv_refs):
        span = slice(part * tokens, (part + 1) * tokens)
        turned = jnp.transpose(kv_ref[...])
        for block in range(BLOCKS):
            start = 2 * C * block
            keys[block, span, :] = kv_ref[:, start : start + C]
            for head in range(HEADS):
                low = start + head * HDIM
                key = turned[low : low + HDIM].astype(F32)
                longest = jnp.max(jnp.sum(key * key, axis=0, keepdims=True))
                largest[block][head] = jnp.maximum(largest[block][head], longest)
                values[block, head, 0:HDIM, span] = turned[low + C : low + C + HDIM]
                values[block, head, HDIM : HDIM + pad, span] = ones
    return largest


def attend(q, keys, values, safe):
    head_row = lax.broadcasted_iota(jnp.int32, q.shape, 0)
    results = []
    for head in range(HEADS):
        mine = (head_row >= head * HDIM) & (head_row < (head + 1) * HDIM)
        scores = dot(keys[...], jnp.where(mine, q, jnp.zeros_like(q)))
        if not safe:
            scores = scores - jnp.max(scores, axis=0, keepdims=True)
        probs = jnp.exp2(scores * SCORE_SCALE).astype(BF16)
        out = dot(values[head], probs)
        results.append(out[:HDIM] * (1.0 / out[HDIM : HDIM + 1]))
    return jnp.concatenate(results, axis=0).astype(BF16)


def within(q, largest):
    square = q.astype(F32)
    square = square * square
    worst = [
        jnp.max(jnp.sum(square[h * HDIM : (h + 1) * HDIM], axis=0, keepdims=True)) * largest[h]
        for h in range(HEADS)
    ]
    return jnp.maximum(worst[0], worst[1]) <= (SAFE_SCORE / SCORE_SCALE) ** 2


def back_kernel(
    edge_ref, _, acc_ref, q_ref, kv_ref, other_ref, field_in, noise_in, gain_in, conv_in,
    query_in, mix_in, out_in, result_ref, keys, values, attended, second, stream, outer, centre,
    packed, flat, acc, queries, field_ref, noise_ref, gain_ref,
    conv_ref, query_ref, mix_ref, out_ref, sems,
):
    span_p, span_e = field_ref.shape[0], field_ref.shape[1]
    width, inner = (span_e + 2) * LAYERS, span_e * LAYERS
    q_copy = pltpu.make_async_copy(q_ref, queries, sems.at[0])
    acc_copy = pltpu.make_async_copy(acc_ref, acc, sems.at[1])
    pairs = [
        (gain_in, gain_ref), (conv_in, conv_ref), (query_in, query_ref), (mix_in, mix_ref),
        (out_in, out_ref), (field_in, field_ref), (noise_in, noise_ref),
    ]
    late = [pltpu.make_async_copy(a, b, sems.at[2 + i]) for i, (a, b) in enumerate(pairs)]
    for copy in [q_copy, acc_copy] + late:
        copy.start()
    largest = prepare_tokens([kv_ref, other_ref], keys, values)
    def attend_rows(source, block, start, rows):
        q = jnp.transpose(source[pl.ds(start, rows), :])
        fine = within(q, largest[block])

        def go(safe):
            found = attend(q, keys.at[block], values.at[block], safe)
            attended[pl.ds(start, rows), :] = jnp.transpose(found)

        pl.when(fine)(lambda: go(True))
        pl.when(jnp.logical_not(fine))(lambda: go(False))

    def attend_all(source, block, count):
        size = TILES[block]
        tiles = count // size

        @pl.loop(0, tiles)
        def _(tile):
            attend_rows(source, block, pl.multiple_of(tile * size, size), size)

        rest = count - tiles * size
        if rest:
            rest = -(-rest // LANES) * LANES
            attend_rows(source, block, count - rest, rest)

    q_copy.wait()
    attend_all(queries, 0, (span_p + 2) * width)
    for copy in [acc_copy] + late:
        copy.wait()
    gain = widened(gain_ref[1:2, :])
    pack_weight(conv_ref, 1, packed)
    for row in range(span_p + 2):
        branch = dot(attended[row * width : (row + 1) * width, :], out_ref[0])
        new = acc[row] + branch
        if 0 < row < span_p + 1:
            stream[row - 1] = new[LAYERS:-LAYERS]
        place = lax.broadcasted_iota(jnp.int32, new.shape, 0)
        outside = ((place < LAYERS) & (edge_ref[0] == 1)) | (
            (place >= width - LAYERS) & (edge_ref[1] == 1)
        )
        normed = normalized(widened(jnp.where(outside, 0.0, new)), gain)
        keep_taps(normed, row, outer, centre)
        if 0 < row < span_p + 1:
            q = dot(centre[row][:, :C], query_ref[1])
            second[(row - 1) * inner : row * inner, :] = q.astype(BF16)

    attend_all(second, 1, span_p * inner)
    for row in range(span_p):
        branch = conv_branch(outer, centre, row, inner, packed, mix_ref[1])
        new = stream[row] + branch + dot(attended[row * inner : (row + 1) * inner, :], out_ref[1])
        flat[...] = widened(new)
        for layer in range(LAYERS):
            last = flat[pl.ds(layer, span_e, stride=LAYERS), :][:, :C]
            span = slice(layer * C, (layer + 1) * C)
            field = field_ref[row, :, span].astype(F32)
            noise = noise_ref[row, :, span].astype(F32)
            result_ref[row, :, span] = (1.02 * (field - 0.2 * last) + 0.3 * noise).astype(BF16)


def back(edges, done, acc, q, kv, other, field, noise, gain, conv_weight, query_weight, mix_weight, out_weight):
    span_p, span_e = field.shape[0], field.shape[1]
    vmem = pl.BlockSpec(memory_space=pltpu.VMEM)
    tokens = kv.shape[0] + other.shape[0]
    rows, width, inner = span_p + 2, (span_e + 2) * LAYERS, span_e * LAYERS
    return pl.pallas_call(
        back_kernel,
        out_shape=jax.ShapeDtypeStruct(field.shape, BF16),
        in_specs=[pl.BlockSpec(memory_space=pltpu.SMEM), pl.BlockSpec(memory_space=pl.ANY)]
        + [pl.BlockSpec(memory_space=pltpu.HBM)] * 2
        + [vmem] * 2
        + [pl.BlockSpec(memory_space=pl.ANY)] * 7,
        out_specs=vmem,
        scratch_shapes=[
            pltpu.VMEM((BLOCKS, tokens, C), BF16),
            pltpu.VMEM((BLOCKS, HEADS, 64, tokens), BF16),
            pltpu.VMEM((rows * width, C), BF16),
            pltpu.VMEM((span_p * inner, C), BF16),
            pltpu.VMEM((span_p, inner, C), F32),
            pltpu.VMEM((rows, width, LANES), BF16),
            pltpu.VMEM((rows, inner, LANES), BF16),
            pltpu.VMEM((9 * LANES, C), BF16),
            pltpu.VMEM((inner, LANES), F32),
            pltpu.VMEM((rows, width, C), F32),
            pltpu.VMEM((rows * width, C), BF16),
            pltpu.VMEM(field.shape, BF16),
            pltpu.VMEM(field.shape, BF16),
            pltpu.VMEM(gain.shape, F32),
            pltpu.VMEM(conv_weight.shape, BF16),
            pltpu.VMEM(query_weight.shape, BF16),
            pltpu.VMEM(mix_weight.shape, BF16),
            pltpu.VMEM(out_weight.shape, BF16),
            pltpu.SemaphoreType.DMA((9,)),
        ],
        compiler_params=pltpu.CompilerParams(vmem_limit_bytes=62_259_200),
        cost_estimate=pl.CostEstimate(
            flops=20_000_000_000, bytes_accessed=6_000_000, transcendentals=21_000_000
        ),
        name="back",
    )(edges, done, acc, q, kv, other, field, noise, gain, conv_weight, query_weight, mix_weight, out_weight)


def tokens_and_front(
    edges, coarse_latent, particle_type, type_table, kv_weight, field, gain, conv_weight,
    query_weight, mix_weight,
):
    local = local_tokens(coarse_latent, particle_type, type_table, kv_weight, len(YZ_GROUPS[0]))
    top, bottom = halo_phi(field)
    west, east = halo_eta(field, top, bottom)
    kv = exchange(local, YZ_GROUPS)
    kv, west, east = lax.optimization_barrier((kv, west, east))
    acc, q, done = front(
        edges, field, top, bottom, west, east, gain, conv_weight, query_weight, mix_weight
    )
    copies = jnp.broadcast_to(kv[None], (len(X_GROUPS[0]),) + kv.shape)
    kv = exchange(copies, X_GROUPS)
    kv, done = lax.optimization_barrier((kv, done))
    other = lax.ppermute(kv, "phi", [(i, i ^ 1) for i in range(lax.axis_size("phi"))])
    return kv, other, acc, q, done


def body(
    noisy_field,
    noise_draw,
    coarse_latent,
    particle_type,
    type_table,
    kv_weight,
    norm_gain,
    conv_weight,
    query_weight,
    mix_weight,
    out_weight,
):
    band = lax.axis_index("eta")
    edges = jnp.stack([band == 0, band == lax.axis_size("eta") - 1]).astype(jnp.int32)
    kv, other, acc, q, done = tokens_and_front(
        edges, coarse_latent, particle_type, type_table, kv_weight, noisy_field, norm_gain,
        conv_weight, query_weight, mix_weight,
    )
    return back(
        edges, done, acc, q, kv, other, noisy_field, noise_draw, norm_gain, conv_weight, query_weight,
        mix_weight, out_weight,
    )


def solution(mesh):
    in_specs = (
        P("phi", "eta", None),
        P("phi", "eta", None),
        P("phi", None),
        P("phi"),
        P(),
        P(),
        P(),
        P(),
        P(),
        P(),
        P(),
    )
    out_specs = P("phi", "eta", None)
    return jax.shard_map(body, mesh=mesh, in_specs=in_specs, out_specs=out_specs, check_vma=False)
```
